32 devices in a mesh: groups: 2 (over x), adapter: 4 (over y, core), tensor: 4 (over z).
Axes of the slice: x: 2, y: 2, z: 4, core: 2. Of those that a mesh axis runs over, the one named last changes fastest.
Arguments:
- tokens: bfloat16 [8192, 8192], P(('groups', 'adapter'), 'tensor'), parts along dimension 0, may hold values from -6 to 6
- shared_weight: bfloat16 [8192, 2048], P('tensor'), may hold values from -0.0625 to 0.0625
- adapter_down_weight: bfloat16 [8192, 2048], P('tensor', 'adapter'), may hold values from -0.0625 to 0.0625
- adapter_up_weight: bfloat16 [2048, 2048], P('adapter', 'tensor'), may hold values from -0.75 to 0.75
- row_adapter_index: int32 [8192], P(('groups', 'adapter')), parts along dimension 0, may hold values from 0 to 31, as said below
Outputs:
- projected: bfloat16 [8192, 2048], P(('groups', 'adapter'), 'tensor'), parts along dimension 0
The draws below stay inside these ranges and needn't reach their ends.
There are 2 independent parts, one for each index of `groups`. The reference program is written for one: setup_inputs(seed, part) draws one part's arguments, and reference() takes and returns one part's arrays. A program takes and returns all parts, laid end to end along the dimension named above; an argument that names none is the same for every part. Nothing has to cross between parts.
Inputs may be any that keep to these rules, and one draw needn't show every extreme that they name: `row_adapter_index`: adapter a is held by the device of index a // 8 along adapter. In every device's block of 1024 rows the rows go to the holders in the same numbers: one holder, the same for the whole part, has exactly 320 of them, and the others share the rest as evenly as possible, so that each has at most 235.
All inputs are finite; a program needn't handle non-finite values.
Results may differ from the reference program's by a relative error of at most 0.014.
Values may be sent and summed in bfloat16 or wider, within the bound.
A program may use at most 128 MiB of HBM per device.

```python
import jax
import jax.numpy as jnp
from jax import lax

MODEL_WIDTH = 8192
PROJECTED_WIDTH = 2048
ADAPTER_RANK = 64
AD_DEV = 8
ROW_DEV = 1024
HOLDERS = 4
ADAPTER_TOTAL = 32
ROWS = 4096
CAP = 320
N_TENSOR = 4


def draw_row_adapter_index(key, part):
    key = jax.random.fold_in(key, 7)
    key_hot, key_other, key_perm, key_local = jax.random.split(key, 4)
    hot_holder = jax.random.randint(key_hot, (), 0, HOLDERS)
    other_holders = (hot_holder + 1 + jax.random.permutation(key_other, HOLDERS - 1)) % HOLDERS
    places = jnp.arange(ROW_DEV)
    later = jnp.maximum(places - CAP, 0) % (HOLDERS - 1)
    layout = jnp.where(places < CAP, hot_holder, other_holders[later])
    block_keys = jax.random.split(key_perm, HOLDERS)

    def shuffle(block_key):
        return layout[jax.random.permutation(block_key, ROW_DEV)]
    holder_rows = jax.vmap(shuffle)(block_keys)
    local_index = jax.random.randint(key_local, (HOLDERS, ROW_DEV), 0, AD_DEV)
    return (holder_rows * AD_DEV + local_index).reshape(ROWS).astype(jnp.int32)


def block_levels(own_key, shape, shards, smallest, largest):
    level, own = 1.0, jax.random.fold_in(own_key, 6)
    for axis_at, parts in shards:
        steps = jnp.exp(jax.random.uniform(jax.random.fold_in(own, axis_at), (parts,), jnp.float32, smallest / len(shards), largest / len(shards)))
        level = level * jnp.repeat(steps, shape[axis_at] // parts).reshape([-1 if axis == axis_at else 1 for axis in range(len(shape))])
    return level


def centred(rng, extent, width, most, cuts=(), held_as=jnp.bfloat16):
    level = block_levels(rng, extent, cuts, -0.22, 0.18) if cuts else 1.0
    drawn = jax.random.normal(rng, extent, jnp.float32) * width * level
    return jnp.minimum(jnp.maximum(drawn, -most), most).astype(held_as)


def setup_inputs(seed: int = 0, part: int = 0) -> dict:
    key_list = jax.random.split(jax.random.key(seed), 6)
    part_keys = jax.random.split(jax.random.fold_in(key_list[5], part), 6)
    return {
        "tokens": centred(part_keys[0], (ROWS, MODEL_WIDTH), 1.0, 6.0, ((0, 4), (1, 4))),
        "shared_weight": centred(key_list[1], (MODEL_WIDTH, PROJECTED_WIDTH), MODEL_WIDTH ** -0.5, 0.0625, ((0, 4),)),
        "adapter_down_weight": centred(key_list[2], (MODEL_WIDTH, ADAPTER_TOTAL * ADAPTER_RANK), MODEL_WIDTH ** -0.5, 0.0625, ((0, 4), (1, 4))),
        "adapter_up_weight": centred(key_list[3], (ADAPTER_TOTAL * ADAPTER_RANK, PROJECTED_WIDTH), ADAPTER_RANK ** -0.5, 0.75, ((0, 4), (1, 4))),
        "row_adapter_index": draw_row_adapter_index(jax.random.fold_in(jax.random.fold_in(key_list[5], part), 71), part),
    }


def reference(tokens, shared_weight, adapter_down_weight, adapter_up_weight, row_adapter_index):
    shard_width = MODEL_WIDTH // N_TENSOR
    base_total = jnp.zeros((tokens.shape[0], PROJECTED_WIDTH), jnp.float32)
    for shard in range(N_TENSOR):
        product = jnp.dot(tokens[:, shard * shard_width:(shard + 1) * shard_width],
                          shared_weight[shard * shard_width:(shard + 1) * shard_width],
                          preferred_element_type=jnp.float32)
        rounded = lax.optimization_barrier(product.astype(jnp.bfloat16))
        base_total = base_total + rounded.astype(jnp.float32)
    sort_order = jnp.argsort(row_adapter_index, stable=True).astype(jnp.int32)
    row_counts = jnp.sum((row_adapter_index[:, None] == jnp.arange(ADAPTER_TOTAL, dtype=jnp.int32)[None, :]).astype(jnp.int32), axis=0).astype(jnp.int32)
    stacked_down_maps = adapter_down_weight.reshape(MODEL_WIDTH, ADAPTER_TOTAL, ADAPTER_RANK).transpose(1, 0, 2)
    stacked_up_maps = adapter_up_weight.reshape(ADAPTER_TOTAL, ADAPTER_RANK, PROJECTED_WIDTH)
    sorted_rows = tokens[sort_order]
    reduced_rows = lax.ragged_dot(sorted_rows, stacked_down_maps, row_counts, preferred_element_type=jnp.float32).astype(jnp.bfloat16)
    delta_rows = lax.ragged_dot(reduced_rows, stacked_up_maps, row_counts, preferred_element_type=jnp.float32).astype(jnp.bfloat16)
    unsorted = jnp.zeros_like(delta_rows).at[sort_order].set(delta_rows)
    return (base_total + unsorted.astype(jnp.float32)).astype(jnp.bfloat16)
```

```python
import functools

import jax
import jax.numpy as jnp
from jax import lax
from jax.experimental import pallas as pl
from jax.experimental.pallas import tpu as pltpu
from jax.sharding import PartitionSpec as P

AD_DEV = 8
RANK = 64
CORES = 2
CHUNKS = 4
PIECES = 2
AHEAD = 3
MESH = pl.DeviceIdType.MESH
BF16 = jnp.bfloat16
F32 = jnp.float32


def kernel(
    G, A, N, C, Q, T,
    tok_h, w_h, down_h, up_h, idx_ref, out_h,
    tok, w, down, up, part, in_r, in_l, idx_col, acc, mine, s_r, s_l, f_r, f_l, total, delta, result,
    load_tok, load_w, load_own, store_out,
    zs_r, zr_r, zs_l, zr_l, ss, sr, ys, yr, xs, xr, os, orr, cs, cr,
):
    Y = A // CORES
    K = (N - 1) * C
    g, a, z = lax.axis_index("groups"), lax.axis_index("adapter"), lax.axis_index("tensor")
    y, core = a // CORES, a % CORES
    R, KD = tok.shape[1], tok.shape[2]
    NB = w.shape[2]
    WD = down.shape[2]
    U = up.shape[1]
    flip = z // (N // 2)

    def block_at(j):
        return (N - 1 - j) * (1 - flip) + j * flip

    def tok_copy(c):
        return pltpu.make_async_copy(tok_h.at[pl.ds(c * R, R)], tok.at[c], load_tok.at[c])

    def w_copy(b):
        columns = pl.ds(pl.multiple_of(b * NB, NB), NB)
        return pltpu.make_async_copy(w_h.at[:, columns], w.at[b], load_w.at[b])

    own_copies = [
        pltpu.make_async_copy(down_h, down.at[a], load_own.at[0]),
        pltpu.make_async_copy(up_h, up.at[a], load_own.at[1]),
    ]
    tok_copy(0).start()
    w_copy(block_at(0)).start()
    for copy in own_copies:
        copy.start()
    for c in range(1, C):
        tok_copy(c).start()
    for j in range(1, N):
        w_copy(block_at(j)).start()

    z_right, z_left = (z + 1) % N, (z + N - 1) % N
    y_next, y_before = ((y + 1) % Y) * CORES + core, ((y + Y - 1) % Y) * CORES + core
    sibling = y * CORES + (CORES - 1 - core)
    greeted = [(g, a, z_right), (g, a, z_left), (g, y_next, z), (g, y_before, z), (g, sibling, z)]
    greeted += [((g + d) % G, a, z) for d in range(1, G)]
    barrier = pltpu.get_barrier_semaphore()
    for device in greeted:
        pl.semaphore_signal(barrier, inc=1, device_id=device, device_id_type=MESH)
    pl.semaphore_wait(barrier, len(greeted))

    def remote(src, dst, send, recv, device):
        return pltpu.make_async_remote_copy(
            src_ref=src, dst_ref=dst, send_sem=send, recv_sem=recv,
            device_id=device, device_id_type=MESH,
        )

    def piece(blk, share, i):
        if i < Q:
            rows = KD // G // Q
            first = pl.multiple_of(share * (KD // G) + i * rows, rows)
            return down.at[blk, pl.ds(first, rows)]
        rows = U // G
        return up.at[blk, pl.ds(pl.multiple_of(share * rows, rows), rows)]

    def y_copy(s, i):
        ref = piece(((y - s + Y) % Y) * CORES + core, g, i)
        return remote(ref, ref, ys.at[s, i], yr.at[s, i], (g, y_next, z))

    def y_landed(s, i):
        ref = piece(((y - s - 1 + Y) % Y) * CORES + core, g, i)
        return remote(ref, ref, ys.at[s, i], yr.at[s, i], (g, y_next, z))

    def x_copy(s, d, i):
        ref = piece(((y - s - 1 + Y) % Y) * CORES + core, g, i)
        return remote(ref, ref, xs.at[s, d - 1, i], xr.at[s, d - 1, i], ((g + d) % G, a, z))

    def x_landed(s, d, i):
        ref = piece(((y - s - 1 + Y) % Y) * CORES + core, (g - d + G) % G, i)
        return remote(ref, ref, xs.at[s, d - 1, i], xr.at[s, d - 1, i], ((g + d) % G, a, z))

    def core_copy(s, d, i, owner):
        ref = piece(((y - s - 1 + Y) % Y) * CORES + owner, (g - d + G) % G, i)
        return remote(ref, ref, cs.at[s, d, i], cr.at[s, d, i], (g, sibling, z))

    def own_copy(i, blk):
        ref = (down if i == 0 else up).at[blk]
        return remote(ref, ref, os.at[i], orr.at[i], (g, sibling, z))

    for i, copy in enumerate(own_copies):
        copy.wait()
        for q in (range(Q) if i == 0 else [Q]):
            y_copy(0, q).start()
        own_copy(i, a).start()

    def send_r(k, src):
        return remote(src, in_r.at[k], zs_r.at[k], zr_r.at[k], (g, a, z_right))

    def send_l(k, src):
        return remote(src, in_l.at[k], zs_l.at[k], zr_l.at[k], (g, a, z_left))

    def product(t, carry):
        j, c = t // C, t % C
        b = block_at(j)

        @pl.when(j == 0)
        def _():
            tok_copy(c).wait()

        @pl.when(c == 0)
        def _():
            w_copy(b).wait()

        part[b, c] = jnp.dot(tok[c], w[b], preferred_element_type=F32).astype(BF16)

        @pl.when((z == 0) & (t < T))
        def _():
            send_r(t, part.at[b, c]).start()

        @pl.when((z == N - 1) & (t < T))
        def _():
            send_l(t, part.at[b, c]).start()

        return carry

    lax.fori_loop(0, N * C, product, 0)

    turned = idx_ref[...].T
    groups_of_rows = idx_ref.shape[0]
    for r in range(groups_of_rows):
        idx_col[pl.ds(r * 128, 128)] = jnp.broadcast_to(turned[:, r:r + 1], (128, 128))

    lane = lax.broadcasted_iota(jnp.int32, (R, 128), 1)
    low = lane < RANK
    half = lane // RANK

    def rows_of(c):
        return pl.ds(pl.multiple_of(c * R, R), R)

    def shrink(blk, first):
        def step(c, carry):
            product = jnp.dot(tok[c], down[blk], preferred_element_type=F32)
            adapter = idx_col[rows_of(c)] - blk * AD_DEV
            kept = jnp.zeros((R, 128), F32)
            for n in range(WD // 128):
                hit = adapter == half + 2 * n
                kept = kept + jnp.where(hit, product[:, n * 128:(n + 1) * 128], 0.0)
            acc[c] = kept if first else acc[c] + kept
            return carry

        lax.fori_loop(0, C, step, 0)

    def pack():
        for c in range(C // 2):
            top, bottom = acc[c], acc[c + C // 2]
            top = top + pltpu.roll(top, RANK, 1)
            bottom = bottom + pltpu.roll(bottom, RANK, 1)
            mine[c] = jnp.where(low, top, bottom).astype(BF16)

    def sum_r(src):
        return remote(src, s_r, ss.at[0], sr.at[0], (g, a, z_right))

    def sum_l(src):
        return remote(src, s_l, ss.at[1], sr.at[1], (g, a, z_left))

    def gather_tasks():
        tasks = []
        for s in range(Y - 1):
            order = [("y", 0), ("y", 1), ("y", 2), ("x", 0), ("x", 1), ("x", 2)]
            tasks += [(kind, s, i) for kind, i in order]
        return tasks

    def run_task(kind, s, i):
        if kind == "y":
            y_landed(s, i).wait_recv()
            if s < Y - 2:
                y_copy(s + 1, i).start()
            for d in range(1, G):
                x_copy(s, d, i).start()
            core_copy(s, 0, i, core).start()
        else:
            for d in range(1, G):
                x_landed(s, d, i).wait_recv()
                core_copy(s, d, i, core).start()

    last = 7 * C // 4
    tasks = gather_tasks()
    places = [1, 3, 4, 4, 5, 6]
    plan = {}
    for n, task in enumerate(tasks):
        at = places[n] * C // 4 if Y == 2 else last
        plan.setdefault(at, []).append(task)

    for k in range(K):
        b_r, b_l, c = N - 1 - k // C, k // C, k % C

        @pl.when(z == 0)
        def _():
            if k >= T:
                send_r(k - T, part.at[N - 1 - (k - T) // C, (k - T) % C]).wait_send()
                send_r(k, part.at[b_r, c]).start()

        @pl.when(z == N - 1)
        def _():
            if k >= T:
                send_l(k - T, part.at[(k - T) // C, (k - T) % C]).wait_send()
                send_l(k, part.at[b_l, c]).start()

        @pl.when((z > 0) & (z < b_r))
        def _():
            send_r(k, in_r.at[k]).wait_recv()
            in_r[k] = (in_r[k].astype(F32) + part[b_r, c].astype(F32)).astype(BF16)
            send_r(k, in_r.at[k]).start()

        @pl.when((z < N - 1) & (z > b_l))
        def _():
            send_l(k, in_l.at[k]).wait_recv()
            in_l[k] = (in_l[k].astype(F32) + part[b_l, c].astype(F32)).astype(BF16)
            send_l(k, in_l.at[k]).start()

        for task in plan.get(k, []):
            run_task(*task)
        if k == C // 4:
            shrink(a, True)
        if k == 2 * C // 4:
            own_copy(0, sibling).wait_recv()
            own_copy(1, sibling).wait_recv()
            shrink(sibling, False)
        if k == last:
            for s in range(Y - 1):
                shrink(((y - s - 1 + Y) % Y) * CORES + core, False)
            for s in range(Y - 1):
                for d in range(G):
                    for i in range(Q + 1):
                        core_copy(s, d, i, CORES - 1 - core).wait_recv()
                shrink(((y - s - 1 + Y) % Y) * CORES + CORES - 1 - core, False)
            pack()

            @pl.when(z == 0)
            def _():
                sum_r(mine).start()

            @pl.when(z == N - 1)
            def _():
                sum_l(mine).start()

    total[...] = mine[...].astype(F32)

    def chain_r():
        @pl.when(z > 0)
        def _():
            sum_r(s_r).wait_recv()
            total[...] += s_r[...].astype(F32)

        @pl.when((z > 0) & (z < N - 1))
        def _():
            f_r[...] = (s_r[...].astype(F32) + mine[...].astype(F32)).astype(BF16)
            sum_r(f_r).start()

    def chain_l():
        @pl.when(z < N - 1)
        def _():
            sum_l(s_l).wait_recv()
            total[...] += s_l[...].astype(F32)

        @pl.when((z > 0) & (z < N - 1))
        def _():
            f_l[...] = (s_l[...].astype(F32) + mine[...].astype(F32)).astype(BF16)
            sum_l(f_l).start()

    @pl.when(flip == 0)
    def _():
        chain_r()
        chain_l()

    @pl.when(flip == 1)
    def _():
        chain_l()
        chain_r()

    def expand(c, carry):
        packed = total[c % (C // 2)]
        rolled = pltpu.roll(packed, RANK, 1)
        upper = (c // (C // 2)) == 0
        keep = low == upper
        both = jnp.where(keep, packed, rolled)
        adapter = idx_col[rows_of(c)]
        sums = jnp.zeros((R, NB), F32)
        for blk in range(A):
            wide = [
                jnp.where(adapter == half + (blk * AD_DEV + 2 * n), both, 0.0).astype(BF16)
                for n in range(U // 128)
            ]
            sums = sums + jnp.dot(
                jnp.concatenate(wide, axis=1), up[blk], preferred_element_type=F32
            )
        delta[c] = sums.astype(BF16)
        return carry

    lax.fori_loop(0, C, expand, 0)

    def out_copy(c):
        return pltpu.make_async_copy(result.at[c], out_h.at[rows_of(c)], store_out.at[c])

    def finish(c, carry):
        k_r, k_l = (N - 1 - z) * C + c, z * C + c

        @pl.when(z == 0)
        def _():
            send_l(k_l, in_l.at[k_l]).wait_recv()
            result[c] = (
                part[z, c].astype(F32) + in_l[k_l].astype(F32) + delta[c].astype(F32)
            ).astype(BF16)

        @pl.when(z == N - 1)
        def _():
            send_r(k_r, in_r.at[k_r]).wait_recv()
            result[c] = (
                part[z, c].astype(F32) + in_r[k_r].astype(F32) + delta[c].astype(F32)
            ).astype(BF16)

        @pl.when((z > 0) & (z < N - 1))
        def _():
            send_l(k_l, in_l.at[k_l]).wait_recv()
            send_r(k_r, in_r.at[k_r]).wait_recv()
            result[c] = (
                part[z, c].astype(F32)
                + in_r[k_r].astype(F32)
                + in_l[k_l].astype(F32)
                + delta[c].astype(F32)
            ).astype(BF16)

        out_copy(c).start()
        return carry

    lax.fori_loop(0, C, finish, 0)

    for k in range(K):
        b_r, b_l = N - 1 - k // C, k // C

        if k >= K - T:
            @pl.when(z == 0)
            def _():
                send_r(k, part.at[b_r, k % C]).wait_send()

            @pl.when(z == N - 1)
            def _():
                send_l(k, part.at[b_l, k % C]).wait_send()

        @pl.when((z > 0) & (z < b_r))
        def _():
            send_r(k, in_r.at[k]).wait_send()

        @pl.when((z < N - 1) & (z > b_l))
        def _():
            send_l(k, in_l.at[k]).wait_send()

    @pl.when(z < N - 1)
    def _():
        sum_r(f_r).wait_send()

    @pl.when(z > 0)
    def _():
        sum_l(f_l).wait_send()

    for i in range(2):
        own_copy(i, a).wait_send()
    for s in range(Y - 1):
        for i in range(Q + 1):
            y_copy(s, i).wait_send()
            for d in range(1, G):
                x_copy(s, d, i).wait_send()
            for d in range(G):
                core_copy(s, d, i, core).wait_send()
    for c in range(C):
        out_copy(c).wait()


def per_device(G, A, N, tokens, shared_weight, adapter_down_weight, adapter_up_weight, row_adapter_index):
    rows, depth = tokens.shape
    C, Q, T = CHUNKS, PIECES, AHEAD
    R = rows // C
    NB = shared_weight.shape[1] // N
    WD = adapter_down_weight.shape[1]
    U = adapter_up_weight.shape[0]
    K = (N - 1) * C
    Y = A // CORES
    DMA = pltpu.SemaphoreType.DMA
    hbm = pl.BlockSpec(memory_space=pl.ANY)
    return pl.pallas_call(
        functools.partial(kernel, G, A, N, C, Q, T),
        out_shape=jax.ShapeDtypeStruct((rows, NB), BF16),
        in_specs=[hbm] * 4 + [pl.BlockSpec(memory_space=pltpu.VMEM)],
        out_specs=hbm,
        scratch_shapes=[
            pltpu.VMEM((C, R, depth), BF16),
            pltpu.VMEM((N, depth, NB), BF16),
            pltpu.VMEM((A, depth, WD), BF16),
            pltpu.VMEM((A, U, NB), BF16),
            pltpu.VMEM((N, C, R, NB), BF16),
            pltpu.VMEM((K, R, NB), BF16),
            pltpu.VMEM((K, R, NB), BF16),
            pltpu.VMEM((rows, 128), jnp.int32),
            pltpu.VMEM((C, R, 128), F32),
            pltpu.VMEM((C // 2, R, 128), BF16),
            pltpu.VMEM((C // 2, R, 128), BF16),
            pltpu.VMEM((C // 2, R, 128), BF16),
            pltpu.VMEM((C // 2, R, 128), BF16),
            pltpu.VMEM((C // 2, R, 128), BF16),
            pltpu.VMEM((C // 2, R, 128), F32),
            pltpu.VMEM((C, R, NB), BF16),
            pltpu.VMEM((C, R, NB), BF16),
            DMA((C,)), DMA((N,)), DMA((2,)), DMA((C,)),
            DMA((K,)), DMA((K,)), DMA((K,)), DMA((K,)),
            DMA((2,)), DMA((2,)),
            DMA((Y - 1, Q + 1)), DMA((Y - 1, Q + 1)),
            DMA((Y - 1, G - 1, Q + 1)), DMA((Y - 1, G - 1, Q + 1)),
            DMA((2,)), DMA((2,)),
            DMA((Y - 1, G, Q + 1)), DMA((Y - 1, G, Q + 1)),
        ],
        compiler_params=pltpu.CompilerParams(
            collective_id=0, has_side_effects=True, vmem_limit_bytes=56 * 2**20
        ),
        cost_estimate=pl.CostEstimate(
            flops=4 * rows * depth * NB * N, bytes_accessed=16 * 2**20, transcendentals=0
        ),
    )(tokens, shared_weight, adapter_down_weight, adapter_up_weight,
      row_adapter_index.reshape(rows // 128, 128))


def solution(mesh):
    in_specs = (
        P(("groups", "adapter"), "tensor"),
        P("tensor", None),
        P("tensor", "adapter"),
        P("adapter", "tensor"),
        P(("groups", "adapter")),
    )
    out_specs = P(("groups", "adapter"), "tensor")
    shape = mesh.shape
    body = functools.partial(per_device, shape["groups"], shape["adapter"], shape["tensor"])
    return jax.shard_map(
        body, mesh=mesh, in_specs=in_specs, out_specs=out_specs, check_vma=False
    )
```

```python
import functools

import jax
import jax.numpy as jnp
from jax import lax
from jax.experimental import pallas as pl
from jax.experimental.pallas import tpu as pltpu
from jax.sharding import PartitionSpec as P

AD_DEV = 8
RANK = 64
CORES = 2
CHUNKS = 8
TILES = 2
PIECES = 4
AHEAD = 4
LAG = 2
MESH = pl.DeviceIdType.MESH
BF16 = jnp.bfloat16
F32 = jnp.float32


def kernel(
    G, A, N, C, Q, T,
    tok_h, w_h, down_h, up_h, idx_ref, out_h,
    tok, w, down, up, part, in_r, in_l, idx_col, acc, mine, s_r, s_l, f_r, f_l, total, delta, result,
    load_tok, load_w, load_own, store_out,
    zs_r, zr_r, zs_l, zr_l, ss, sr, ys, yr, xs, xr, os, orr, cs, cr,
):
    Y = A // CORES
    K = (N - 1) * C
    g, a, z = lax.axis_index("groups"), lax.axis_index("adapter"), lax.axis_index("tensor")
    y, core = a // CORES, a % CORES
    M, KD = tok.shape[1], tok.shape[2]
    R = part.shape[2]
    B = tok.shape[0]
    S = C // B
    NB = w.shape[2]
    WD = down.shape[2]
    U = up.shape[1]
    flip = z // (N // 2)

    def block_at(j):
        return (N - 1 - j) * (1 - flip) + j * flip

    def tok_copy(c):
        return pltpu.make_async_copy(tok_h.at[pl.ds(c * M, M)], tok.at[c], load_tok.at[c])

    def w_copy(b):
        columns = pl.ds(pl.multiple_of(b * NB, NB), NB)
        return pltpu.make_async_copy(w_h.at[:, columns], w.at[b], load_w.at[b])

    own_copies = [
        pltpu.make_async_copy(down_h, down.at[a], load_own.at[0]),
        pltpu.make_async_copy(up_h, up.at[a], load_own.at[1]),
    ]
    tok_copy(0).start()
    w_copy(block_at(0)).start()
    for copy in own_copies:
        copy.start()
    for c in range(1, B):
        tok_copy(c).start()
    for j in range(1, N):
        w_copy(block_at(j)).start()

    z_right, z_left = (z + 1) % N, (z + N - 1) % N
    y_next, y_before = ((y + 1) % Y) * CORES + core, ((y + Y - 1) % Y) * CORES + core
    sibling = y * CORES + (CORES - 1 - core)
    greeted = [(g, a, z_right), (g, a, z_left), (g, y_next, z), (g, y_before, z), (g, sibling, z)]
    greeted += [((g + d) % G, a, z) for d in range(1, G)]
    barrier = pltpu.get_barrier_semaphore()
    for device in greeted:
        pl.semaphore_signal(barrier, inc=1, device_id=device, device_id_type=MESH)
    pl.semaphore_wait(barrier, len(greeted))

    def remote(src, dst, send, recv, device):
        return pltpu.make_async_remote_copy(
            src_ref=src, dst_ref=dst, send_sem=send, recv_sem=recv,
            device_id=device, device_id_type=MESH,
        )

    def piece(blk, share, i):
        if i < Q:
            rows = KD // G // Q
            first = pl.multiple_of(share * (KD // G) + i * rows, rows)
            return down.at[blk, pl.ds(first, rows)]
        rows = U // G
        return up.at[blk, pl.ds(pl.multiple_of(share * rows, rows), rows)]

    def y_copy(s, i):
        ref = piece(((y - s + Y) % Y) * CORES + core, g, i)
        return remote(ref, ref, ys.at[s, i], yr.at[s, i], (g, y_next, z))

    def y_landed(s, i):
        ref = piece(((y - s - 1 + Y) % Y) * CORES + core, g, i)
        return remote(ref, ref, ys.at[s, i], yr.at[s, i], (g, y_next, z))

    def x_copy(s, d, i):
        ref = piece(((y - s - 1 + Y) % Y) * CORES + core, g, i)
        return remote(ref, ref, xs.at[s, d - 1, i], xr.at[s, d - 1, i], ((g + d) % G, a, z))

    def x_landed(s, d, i):
        ref = piece(((y - s - 1 + Y) % Y) * CORES + core, (g - d + G) % G, i)
        return remote(ref, ref, xs.at[s, d - 1, i], xr.at[s, d - 1, i], ((g + d) % G, a, z))

    def core_copy(s, d, i, owner):
        ref = piece(((y - s - 1 + Y) % Y) * CORES + owner, (g - d + G) % G, i)
        return remote(ref, ref, cs.at[s, d, i], cr.at[s, d, i], (g, sibling, z))

    def own_copy(i, blk):
        ref = (down if i == 0 else up).at[blk]
        return remote(ref, ref, os.at[i], orr.at[i], (g, sibling, z))

    for i, copy in enumerate(own_copies):
        copy.wait()
        for q in (range(Q) if i == 0 else [Q]):
            y_copy(0, q).start()
        own_copy(i, a).start()

    def send_r(k, src):
        return remote(src, in_r.at[k], zs_r.at[k], zr_r.at[k], (g, a, z_right))

    def send_l(k, src):
        return remote(src, in_l.at[k], zs_l.at[k], zr_l.at[k], (g, a, z_left))

    def product(t, carry):
        j, m = t // B, t % B
        b = block_at(j)

        @pl.when(j == 0)
        def _():
            tok_copy(m).wait()

        @pl.when(m == 0)
        def _():
            w_copy(b).wait()

        dense = jnp.dot(tok[m], w[b], preferred_element_type=F32).astype(BF16)
        for i in range(S):
            part[b, m * S + i] = dense[i * R:(i + 1) * R]

        for i in range(S):
            k = t * S + i

            @pl.when((z == 0) & (k < T))
            def _():
                send_r(k, part.at[b, m * S + i]).start()

            @pl.when((z == N - 1) & (k < T))
            def _():
                send_l(k, part.at[b, m * S + i]).start()

        return carry

    lax.fori_loop(0, N * B, product, 0)

    turned = idx_ref[...].T
    groups_of_rows = idx_ref.shape[0]
    for r in range(groups_of_rows):
        idx_col[pl.ds(r * 128, 128)] = jnp.broadcast_to(turned[:, r:r + 1], (128, 128))

    lane = lax.broadcasted_iota(jnp.int32, (M, 128), 1)
    low = lane < RANK
    half = lane // RANK

    def rows_of(c):
        return pl.ds(pl.multiple_of(c * R, R), R)

    def rows_of_tile(m):
        return pl.ds(pl.multiple_of(m * M, M), M)

    def shrink(blk, first):
        def step(m, carry):
            product = jnp.dot(tok[m], down[blk], preferred_element_type=F32)
            adapter = idx_col[rows_of_tile(m)] - blk * AD_DEV
            kept = jnp.zeros((M, 128), F32)
            for n in range(WD // 128):
                hit = adapter == half + 2 * n
                kept = kept + jnp.where(hit, product[:, n * 128:(n + 1) * 128], 0.0)
            acc[m] = kept if first else acc[m] + kept
            return carry

        lax.fori_loop(0, B, step, 0)

    def pack():
        for c in range(B // 2):
            top, bottom = acc[c], acc[c + B // 2]
            top = top + pltpu.roll(top, RANK, 1)
            bottom = bottom + pltpu.roll(bottom, RANK, 1)
            mine[c] = jnp.where(low, top, bottom).astype(BF16)

    def sum_r(src):
        return remote(src, s_r, ss.at[0], sr.at[0], (g, a, z_right))

    def sum_l(src):
        return remote(src, s_l, ss.at[1], sr.at[1], (g, a, z_left))

    def run_task(kind, s, i):
        if kind == "y":
            y_landed(s, i).wait_recv()
            if s < Y - 2:
                y_copy(s + 1, i).start()
            for d in range(1, G):
                x_copy(s, d, i).start()
            core_copy(s, 0, i, core).start()
        else:
            for d in range(1, G):
                x_landed(s, d, i).wait_recv()
                core_copy(s, d, i, core).start()

    last = min(2 * C, K - 1)
    order = []
    for s in range(Y - 1):
        order += [("y", s, 0)]
        for i in range(1, Q + 1):
            order += [("y", s, i), ("x", s, i - 1)]
        order += [("x", s, Q)]
    plan_end, plan_middle = {}, {}
    for n, task in enumerate(order):
        i = task[2] + (1 if task[0] == "x" else 0)
        for plan, first in ((plan_end, T), (plan_middle, 0)):
            at = min(first + 2 * i + 1, last) if Y == 2 else last
            plan.setdefault(at, []).append(task)

    def forward_r(k):
        b_r, c = N - 1 - k // C, k % C

        @pl.when((z > 0) & (z < b_r))
        def _():
            send_r(k, in_r.at[k]).wait_recv()
            in_r[k] = (in_r[k].astype(F32) + part[b_r, c].astype(F32)).astype(BF16)
            send_r(k, in_r.at[k]).start()

    def forward_l(k):
        b_l, c = k // C, k % C

        @pl.when((z < N - 1) & (z > b_l))
        def _():
            send_l(k, in_l.at[k]).wait_recv()
            in_l[k] = (in_l[k].astype(F32) + part[b_l, c].astype(F32)).astype(BF16)
            send_l(k, in_l.at[k]).start()

    for k in range(K):
        b_r, b_l, c = N - 1 - k // C, k // C, k % C

        @pl.when(z == 0)
        def _():
            if k >= T:
                send_r(k - T, part.at[N - 1 - (k - T) // C, (k - T) % C]).wait_send()
                send_r(k, part.at[b_r, c]).start()

        @pl.when(z == N - 1)
        def _():
            if k >= T:
                send_l(k - T, part.at[(k - T) // C, (k - T) % C]).wait_send()
                send_l(k, part.at[b_l, c]).start()

        @pl.when(flip == 0)
        def _():
            forward_r(k)
            if k >= LAG:
                forward_l(k - LAG)

        @pl.when(flip == 1)
        def _():
            forward_l(k)
            if k >= LAG:
                forward_r(k - LAG)

        if k in plan_end:
            @pl.when((z == 0) | (z == N - 1))
            def _():
                for task in plan_end[k]:
                    run_task(*task)

        if k in plan_middle:
            @pl.when((z > 0) & (z < N - 1))
            def _():
                for task in plan_middle[k]:
                    run_task(*task)

        if k == C // 2:
            shrink(a, True)
        if k == 3 * C // 4:
            own_copy(0, sibling).wait_recv()
            own_copy(1, sibling).wait_recv()
            shrink(sibling, False)
        if k == last:
            for s in range(Y - 1):
                shrink(((y - s - 1 + Y) % Y) * CORES + core, False)
            for s in range(Y - 1):
                for d in range(G):
                    for i in range(Q + 1):
                        core_copy(s, d, i, CORES - 1 - core).wait_recv()
                shrink(((y - s - 1 + Y) % Y) * CORES + CORES - 1 - core, False)
            pack()

            @pl.when(z == 0)
            def _():
                sum_r(mine).start()

            @pl.when(z == N - 1)
            def _():
                sum_l(mine).start()

    total[...] = mine[...].astype(F32)

    def chain_r():
        @pl.when(z > 0)
        def _():
            sum_r(s_r).wait_recv()
            total[...] += s_r[...].astype(F32)

        @pl.when((z > 0) & (z < N - 1))
        def _():
            f_r[...] = (s_r[...].astype(F32) + mine[...].astype(F32)).astype(BF16)
            sum_r(f_r).start()

    def chain_l():
        @pl.when(z < N - 1)
        def _():
            sum_l(s_l).wait_recv()
            total[...] += s_l[...].astype(F32)

        @pl.when((z > 0) & (z < N - 1))
        def _():
            f_l[...] = (s_l[...].astype(F32) + mine[...].astype(F32)).astype(BF16)
            sum_l(f_l).start()

    @pl.when(flip == 0)
    def _():
        chain_r()
        chain_l()

    @pl.when(flip == 1)
    def _():
        chain_l()
        chain_r()

    def expand(m, carry):
        packed = total[m % (B // 2)]
        rolled = pltpu.roll(packed, RANK, 1)
        upper = (m // (B // 2)) == 0
        keep = low == upper
        both = jnp.where(keep, packed, rolled)
        adapter = idx_col[rows_of_tile(m)]
        sums = jnp.zeros((M, NB), F32)
        for blk in range(A):
            wide = [
                jnp.where(adapter == half + (blk * AD_DEV + 2 * n), both, 0.0).astype(BF16)
                for n in range(U // 128)
            ]
            sums = sums + jnp.dot(
                jnp.concatenate(wide, axis=1), up[blk], preferred_element_type=F32
            )
        sums = sums.astype(BF16)
        for i in range(S):
            delta[m * S + i] = sums[i * R:(i + 1) * R]
        return carry

    lax.fori_loop(0, B, expand, 0)

    def out_copy(c):
        return pltpu.make_async_copy(result.at[c], out_h.at[rows_of(c)], store_out.at[c])

    def finish(c, carry):
        k_r, k_l = (N - 1 - z) * C + c, z * C + c

        @pl.when(z == 0)
        def _():
            send_l(k_l, in_l.at[k_l]).wait_recv()
            result[c] = (
                part[z, c].astype(F32) + in_l[k_l].astype(F32) + delta[c].astype(F32)
            ).astype(BF16)

        @pl.when(z == N - 1)
        def _():
            send_r(k_r, in_r.at[k_r]).wait_recv()
            result[c] = (
                part[z, c].astype(F32) + in_r[k_r].astype(F32) + delta[c].astype(F32)
            ).astype(BF16)

        @pl.when((z > 0) & (z < N - 1))
        def _():
            send_l(k_l, in_l.at[k_l]).wait_recv()
            send_r(k_r, in_r.at[k_r]).wait_recv()
            result[c] = (
                part[z, c].astype(F32)
                + in_r[k_r].astype(F32)
                + in_l[k_l].astype(F32)
                + delta[c].astype(F32)
            ).astype(BF16)

        out_copy(c).start()
        return carry

    lax.fori_loop(0, C, finish, 0)

    for k in range(K):
        b_r, b_l = N - 1 - k // C, k // C

        if k >= K - T:
            @pl.when(z == 0)
            def _():
                send_r(k, part.at[b_r, k % C]).wait_send()

            @pl.when(z == N - 1)
            def _():
                send_l(k, part.at[b_l, k % C]).wait_send()

        @pl.when((z > 0) & (z < b_r))
        def _():
            send_r(k, in_r.at[k]).wait_send()

        @pl.when((z < N - 1) & (z > b_l))
        def _():
            send_l(k, in_l.at[k]).wait_send()

    @pl.when(z < N - 1)
    def _():
        sum_r(f_r).wait_send()

    @pl.when(z > 0)
    def _():
        sum_l(f_l).wait_send()

    for i in range(2):
        own_copy(i, a).wait_send()
    for s in range(Y - 1):
        for i in range(Q + 1):
            y_copy(s, i).wait_send()
            for d in range(1, G):
                x_copy(s, d, i).wait_send()
            for d in range(G):
                core_copy(s, d, i, core).wait_send()
    for c in range(C):
        out_copy(c).wait()


def per_device(G, A, N, tokens, shared_weight, adapter_down_weight, adapter_up_weight, row_adapter_index):
    rows, depth = tokens.shape
    C, B, Q, T = CHUNKS, TILES, PIECES, AHEAD
    R, M = rows // C, rows // B
    NB = shared_weight.shape[1] // N
    WD = adapter_down_weight.shape[1]
    U = adapter_up_weight.shape[0]
    K = (N - 1) * C
    Y = A // CORES
    DMA = pltpu.SemaphoreType.DMA
    hbm = pl.BlockSpec(memory_space=pl.ANY)
    return pl.pallas_call(
        functools.partial(kernel, G, A, N, C, Q, T),
        out_shape=jax.ShapeDtypeStruct((rows, NB), BF16),
        in_specs=[hbm] * 4 + [pl.BlockSpec(memory_space=pltpu.VMEM)],
        out_specs=hbm,
        scratch_shapes=[
            pltpu.VMEM((B, M, depth), BF16),
            pltpu.VMEM((N, depth, NB), BF16),
            pltpu.VMEM((A, depth, WD), BF16),
            pltpu.VMEM((A, U, NB), BF16),
            pltpu.VMEM((N, C, R, NB), BF16),
            pltpu.VMEM((K, R, NB), BF16),
            pltpu.VMEM((K, R, NB), BF16),
            pltpu.VMEM((rows, 128), jnp.int32),
            pltpu.VMEM((B, M, 128), F32),
            pltpu.VMEM((B // 2, M, 128), BF16),
            pltpu.VMEM((B // 2, M, 128), BF16),
            pltpu.VMEM((B // 2, M, 128), BF16),
            pltpu.VMEM((B // 2, M, 128), BF16),
            pltpu.VMEM((B // 2, M, 128), BF16),
            pltpu.VMEM((B // 2, M, 128), F32),
            pltpu.VMEM((C, R, NB), BF16),
            pltpu.VMEM((C, R, NB), BF16),
            DMA((B,)), DMA((N,)), DMA((2,)), DMA((C,)),
            DMA((K,)), DMA((K,)), DMA((K,)), DMA((K,)),
            DMA((2,)), DMA((2,)),
            DMA((Y - 1, Q + 1)), DMA((Y - 1, Q + 1)),
            DMA((Y - 1, G - 1, Q + 1)), DMA((Y - 1, G - 1, Q + 1)),
            DMA((2,)), DMA((2,)),
            DMA((Y - 1, G, Q + 1)), DMA((Y - 1, G, Q + 1)),
        ],
        compiler_params=pltpu.CompilerParams(
            collective_id=0, has_side_effects=True, vmem_limit_bytes=56 * 2**20
        ),
        cost_estimate=pl.CostEstimate(
            flops=4 * rows * depth * NB * N, bytes_accessed=16 * 2**20, transcendentals=0
        ),
    )(tokens, shared_weight, adapter_down_weight, adapter_up_weight,
      row_adapter_index.reshape(rows // 128, 128))


def solution(mesh):
    in_specs = (
        P(("groups", "adapter"), "tensor"),
        P("tensor", None),
        P("tensor", "adapter"),
        P("adapter", "tensor"),
        P(("groups", "adapter")),
    )
    out_specs = P(("groups", "adapter"), "tensor")
    shape = mesh.shape
    body = functools.partial(per_device, shape["groups"], shape["adapter"], shape["tensor"])
    return jax.shard_map(
        body, mesh=mesh, in_specs=in_specs, out_specs=out_specs, check_vma=False
    )
```
